32 devices in a mesh: groups: 2 (over x), gx: 16 (over z, y, core).
Axes of the slice: x: 2, y: 2, z: 4, core: 2. Of those that a mesh axis runs over, the one named last changes fastest.
Arguments:
- features: bfloat16 [32, 256, 16, 128], P(None, ('groups', 'gx')), parts along dimension 1, may hold values from -6 to 6
- active_blocks: int32 [32, 2, 16], P(('groups', 'gx')), parts along dimension 0, may hold values 0 or 1
- weight_fine: bfloat16 [32, 32, 3, 3, 3], replicated, may hold values from -0.21875 to 0.21875
- weight_coarse: bfloat16 [64, 32, 3, 3, 3], replicated, may hold values from -0.21875 to 0.21875
- weight_up: bfloat16 [32, 64], replicated, may hold values from -0.75 to 0.75
- cotangent: bfloat16 [32, 256, 16, 128], P(None, ('groups', 'gx')), parts along dimension 1, may hold values from -6 to 6
Outputs:
- net_output: bfloat16 [32, 256, 16, 128], P(None, ('groups', 'gx')), parts along dimension 1
- grad_features: float32 [32, 256, 16, 128], P(None, ('groups', 'gx')), parts along dimension 1
- grad_fine: float32 [64, 32, 3, 3, 3], P('groups'), parts along dimension 0
- grad_coarse: float32 [128, 32, 3, 3, 3], P('groups'), parts along dimension 0
- grad_up: float32 [64, 64], P('groups'), parts along dimension 0
The draws below stay inside these ranges and needn't reach their ends.
There are 2 independent parts, one for each index of `groups`. The reference program is written for one: setup_inputs(seed, part) draws one part's arguments, and reference() takes and returns one part's arrays. A program takes and returns all parts, laid end to end along the dimension named above; an argument that names none is the same for every part. Nothing has to cross between parts.
All inputs are finite; a program needn't handle non-finite values. No bound on the sum of `active_blocks` on one device may be relied on, other than what follows from the above.
Results may differ from the reference program's by a relative error of at most 0.01.
Values may be sent and summed in bfloat16 or wider, within the bound.
A program may use at most 128 MiB of HBM per device.

```python
import math
import jax
import jax.numpy as jnp
from jax import lax

C0 = 32
C1 = 64
NZ = 16
NY = 128
NX = 128


def with_ends(result, key, low, high):
    longest = result.shape.index(max(result.shape))
    spots = []
    for shift in (0, 1):
        where = [jax.random.randint(jax.random.fold_in(key, axis), (), 0, length) for axis, length in enumerate(result.shape)]
        where[longest] = (where[longest] + shift) % result.shape[longest]
        spots.append(tuple(where))
    return result.at[spots[0]].set(low).at[spots[1]].set(high)


def level_of(rng, shape, split, low, top_value):
    level = 1.0
    for position, shards_of in split:
        steps = jax.random.uniform(jax.random.fold_in(jax.random.fold_in(rng, 6), position), (shards_of,), jnp.float32, low / len(split), top_value / len(split))
        level = level * jnp.repeat(jnp.exp(steps), shape[position] // shards_of).reshape((-1,) + (1,) * (len(shape) - 1 - position))
    return level


def scatter_about(own_key, shape, width, limit, pieces=(), dtype=jnp.bfloat16):
    factor_of = level_of(own_key, shape, pieces, -0.22, 0.18) if pieces else 1.0
    array = jax.random.normal(own_key, shape, jnp.float32) * width * factor_of
    return jnp.minimum(jnp.maximum(array, -limit), limit).astype(dtype)


def setup_inputs(seed: int = 0, part: int = 0) -> dict:
    streams_of = jax.random.split(jax.random.key(seed), 7)
    part_keys = jax.random.split(jax.random.fold_in(streams_of[6], part), 7)
    return {
        "features": scatter_about(part_keys[0], (C0, NX, NZ, NY), 1.0, 6.0, ((1, 16),)),
        "active_blocks": with_ends((jax.random.randint(part_keys[1], (NX // 8, NZ // 8, NY // 8), 0, 4) < 3).astype(jnp.int32), jax.random.fold_in(part_keys[1], 1), 0, 1),
        "weight_fine": scatter_about(streams_of[2], (C0, C0, 3, 3, 3), (27 * C0) ** -0.5, 0.21875),
        "weight_coarse": scatter_about(streams_of[3], (C1, C0, 3, 3, 3), (27 * C0) ** -0.5, 0.21875),
        "weight_up": scatter_about(streams_of[4], (C0, C1), C1 ** -0.5, 0.75),
        "cotangent": scatter_about(part_keys[5], (C0, NX, NZ, NY), 1.0, 6.0, ((1, 16),)),
    }


dimension_names = ('NCDHW', 'OIDHW', 'NCDHW')

def conv_rows(padded, weight):
    return lax.conv_general_dilated(padded[None], weight, (1, 1, 1), [(0, 0), (1, 1), (1, 1)], dimension_numbers=dimension_names, preferred_element_type=jnp.float32)[0]

def conv_back(grad, weight):
    flipped = jnp.flip(weight, (2, 3, 4)).transpose(1, 0, 2, 3, 4)
    return lax.conv_general_dilated(grad[None], flipped, (1, 1, 1), [(2, 2), (1, 1), (1, 1)], dimension_numbers=dimension_names, preferred_element_type=jnp.float32)[0]

def weight_grad(padded, grad):
    widened = jnp.pad(padded, ((0, 0), (0, 0), (1, 1), (1, 1))).astype(jnp.float32)
    grad_wide = grad.astype(jnp.float32)
    extent_x, extent_z, extent_y = (grad.shape[1], grad.shape[2], grad.shape[3])
    tap_list = []
    for i in range(3):
        for j in range(3):
            for k in range(3):
                window = widened[:, i:i + extent_x, j:j + extent_z, k:k + extent_y]
                tap_list.append(jnp.einsum('oxzy,cxzy->oc', grad_wide, window, precision=lax.Precision.HIGHEST))
    stacked = jnp.stack(tap_list, axis=2)
    return stacked.reshape(stacked.shape[0], stacked.shape[1], 3, 3, 3)

def expand_mask(blocks, factor):
    values = blocks.astype(jnp.float32)
    size_x, size_z, size_y = values.shape
    values = jnp.broadcast_to(values[:, None, :, None, :, None], (size_x, factor, size_z, factor, size_y, factor))
    return values.reshape(size_x * factor, size_z * factor, size_y * factor)

def pool_sum(values):
    chans, size_x, size_z, size_y = values.shape
    return values.reshape(chans, size_x // 2, 2, size_z // 2, 2, size_y // 2, 2).sum(axis=(2, 4, 6))

def spread(values):
    chans, size_x, size_z, size_y = values.shape
    wide_view = jnp.broadcast_to(values[:, :, None, :, None, :, None], (chans, size_x, 2, size_z, 2, size_y, 2))
    return wide_view.reshape(chans, size_x * 2, size_z * 2, size_y * 2)

def silu_slope(values):
    sigma = jax.nn.sigmoid(values)
    return sigma * (1.0 + values * (1.0 - sigma))

def reference(features, active_blocks, weight_fine, weight_coarse, weight_up, cotangent):
    factor = 1.0 / math.sqrt(NX * NZ * NY)
    fine_mask = expand_mask(active_blocks, 8)
    coarse_mask = expand_mask(active_blocks, 4)
    padded = jnp.pad(features, ((0, 0), (1, 1), (0, 0), (0, 0)))
    pre_fine = conv_rows(padded, weight_fine)
    hidden_fine = (jax.nn.silu(pre_fine) * fine_mask).astype(jnp.bfloat16)
    pooled = (pool_sum(hidden_fine.astype(jnp.float32)) * 0.125).astype(jnp.bfloat16)
    pooled_pad = jnp.pad(pooled, ((0, 0), (1, 1), (0, 0), (0, 0)))
    pre_coarse = conv_rows(pooled_pad, weight_coarse)
    hidden_coarse = (jax.nn.silu(pre_coarse) * coarse_mask).astype(jnp.bfloat16)
    lifted = jnp.einsum('oc,cxzy->oxzy', weight_up.astype(jnp.float32), hidden_coarse.astype(jnp.float32), precision=lax.Precision.HIGHEST)
    net_output = (hidden_fine.astype(jnp.float32) + fine_mask * spread(lifted)).astype(jnp.bfloat16)
    grad_lift = pool_sum(cotangent.astype(jnp.float32) * fine_mask)
    grad_up = factor * jnp.einsum('oxzy,cxzy->oc', grad_lift, hidden_coarse.astype(jnp.float32), precision=lax.Precision.HIGHEST)
    grad_hidden_coarse = jnp.einsum('oc,oxzy->cxzy', weight_up.astype(jnp.float32), grad_lift, precision=lax.Precision.HIGHEST)
    grad_pre_coarse = (grad_hidden_coarse * coarse_mask * silu_slope(pre_coarse)).astype(jnp.bfloat16)
    grad_coarse = factor * weight_grad(pooled_pad, grad_pre_coarse)
    grad_pooled = conv_back(grad_pre_coarse, weight_coarse)[:, 1:-1]
    grad_hidden = cotangent.astype(jnp.float32) + spread(grad_pooled) * 0.125
    grad_pre_fine = (grad_hidden * fine_mask * silu_slope(pre_fine)).astype(jnp.bfloat16)
    grad_fine = factor * weight_grad(padded, grad_pre_fine)
    grad_features = conv_back(grad_pre_fine, weight_fine)[:, 1:-1]
    return (net_output, grad_features, grad_fine, grad_coarse, grad_up)
```

```python
import functools
import math

import jax
import jax.numpy as jnp
import numpy as np
from jax import lax
from jax.experimental import pallas as pl
from jax.experimental.pallas import tpu as pltpu
from jax.sharding import PartitionSpec as P

F32 = jnp.float32
BF16 = jnp.bfloat16
VMEM_LIMIT = 48 * 1024 * 1024
MESH = pl.DeviceIdType.MESH
ALONG = 4


def dot(a, b):
    return jnp.dot(a, b, preferred_element_type=F32)


def dot_nt(a, b):
    return lax.dot_general(a, b, (((1,), (1,)), ((), ())), preferred_element_type=F32)


def halves(value):
    high = value.astype(BF16)
    return high, (value - high.astype(F32)).astype(BF16)


def pool_matrix(size_y):
    cell = np.arange(4 * size_y)
    coarse = np.arange(size_y)
    same_z = (cell // size_y // 2)[:, None] == (coarse // (size_y // 2))[None]
    same_y = (cell % size_y // 2)[:, None] == (coarse % (size_y // 2))[None]
    return (same_z & same_y).astype(np.float32)


def gather_fine(value, size_y, cols_ref, row):
    chans, length = value.shape
    wide = value.astype(F32)
    spot = lax.broadcasted_iota(jnp.int32, (chans, length), 1) % size_y
    before = jnp.where(spot == 0, 0.0, pltpu.roll(wide, 1, 1)).astype(BF16)
    after = jnp.where(spot == size_y - 1, 0.0, pltpu.roll(wide, length - 1, 1)).astype(BF16)
    edge = jnp.zeros((chans, size_y), BF16)
    for k, shifted in enumerate((before, value, after)):
        low = pl.ds(row + k * chans, chans)
        mid = pl.ds(row + (3 + k) * chans, chans)
        high = pl.ds(row + (6 + k) * chans, chans)
        cols_ref[low, :size_y] = edge
        cols_ref[low, size_y:] = shifted[:, :-size_y]
        cols_ref[mid, :] = shifted
        cols_ref[high, : length - size_y] = shifted[:, size_y:]
        cols_ref[high, length - size_y :] = edge


def gather_coarse(value, size_y, cols_ref, row):
    chans, length = value.shape
    wide = value.astype(F32)
    cell = lax.broadcasted_iota(jnp.int32, (chans, length), 1)
    spot = cell % size_y
    for j in range(3):
        for k in range(3):
            shift = (j - 1) * size_y + (k - 1)
            rolled = pltpu.roll(wide, (-shift) % length, 1) if shift else wide
            if k == 0:
                rolled = jnp.where(spot == 0, 0.0, rolled)
            if k == 2:
                rolled = jnp.where(spot == size_y - 1, 0.0, rolled)
            if j == 0:
                rolled = jnp.where(cell < size_y, 0.0, rolled)
            if j == 2:
                rolled = jnp.where(cell >= length - size_y, 0.0, rolled)
            cols_ref[pl.ds(row + (3 * j + k) * chans, chans), :] = rolled.astype(BF16)


def gather_planes(gather, low_ref, mid_ref, high_ref, chans, size_y, cols_ref):
    planes = mid_ref.shape[0] // chans
    depth = 9 * chans
    gather(low_ref[...], size_y, cols_ref, 0)
    gather(high_ref[...], size_y, cols_ref, (planes + 1) * depth)

    def body(plane, carry):
        start = pl.multiple_of(plane * chans, chans)
        row = pl.multiple_of((plane + 1) * depth, depth)
        gather(mid_ref[pl.ds(start, chans), :], size_y, cols_ref, row)
        return carry

    lax.fori_loop(0, planes, body, 0)


def sum_pairs(value, chans):
    count = value.shape[0] // chans
    return jnp.concatenate(
        [
            value[(2 * i) * chans : (2 * i + 1) * chans]
            + value[(2 * i + 1) * chans : (2 * i + 2) * chans]
            for i in range(count // 2)
        ],
        axis=0,
    )


def repeat_pairs(value, chans):
    count = value.shape[0] // chans
    parts = [value[i // 2 * chans : (i // 2 + 1) * chans] for i in range(2 * count)]
    return jnp.concatenate(parts, axis=0)


def sigmoid(value):
    return 1.0 / (1.0 + jnp.exp(-value))


def fine_forward(
    size_y, low_ref, mid_ref, high_ref, taps_ref, mask_ref, pool_ref,
    hidden_ref, slope_ref, pooled_ref, cols_ref,
):
    chans = low_ref.shape[0]
    length = mid_ref.shape[1]
    gather_planes(gather_fine, low_ref, mid_ref, high_ref, chans, size_y, cols_ref)
    depth = 9 * chans
    wide = 4 * size_y
    for group in range(mid_ref.shape[0] // chans // ALONG):
        rows = slice(group * ALONG * depth, (group * ALONG + ALONG + 2) * depth)
        held = slice(group * ALONG * chans, (group + 1) * ALONG * chans)
        out = slice(group * ALONG // 2 * chans, (group + 1) * ALONG // 2 * chans)
        for step in range(length // wide):
            lanes = slice(step * wide, (step + 1) * wide)
            pre = dot(taps_ref[...], cols_ref[rows, lanes])
            mask = mask_ref[:, lanes]
            sigma = sigmoid(pre)
            hidden = (pre * sigma * mask).astype(BF16)
            hidden_ref[held, lanes] = hidden
            slope_ref[held, lanes] = sigma * (1.0 + pre * (1.0 - sigma)) * mask
            pooled = sum_pairs(dot(hidden, pool_ref[...]), chans) * 0.125
            pooled_ref[out, step * size_y : (step + 1) * size_y] = pooled.astype(BF16)


def lift_pool(size_y, chans, cotangent_ref, mask_ref, pool_ref, lift_ref):
    wide = 4 * size_y
    for step in range(cotangent_ref.shape[1] // wide):
        lanes = slice(step * wide, (step + 1) * wide)
        value = (cotangent_ref[:, lanes].astype(F32) * mask_ref[:, lanes]).astype(BF16)
        lift_ref[:, step * size_y : (step + 1) * size_y] = sum_pairs(
            dot(value, pool_ref[...]), chans
        )


def coarse_forward(
    size_y, low_ref, mid_ref, high_ref, taps_ref, mask_ref, lift_ref, back_ref,
    hidden_ref, grad_ref, cols_ref,
):
    chans = low_ref.shape[0]
    gather_planes(gather_coarse, low_ref, mid_ref, high_ref, chans, size_y, cols_ref)
    pre = dot(taps_ref[...], cols_ref[...])
    mask = mask_ref[...]
    sigma = sigmoid(pre)
    hidden_ref[...] = (pre * sigma * mask).astype(BF16)
    high, low = halves(lift_ref[...])
    lifted = dot(back_ref[...], high) + dot(back_ref[...], low)
    slope = sigma * (1.0 + pre * (1.0 - sigma))
    grad_ref[...] = (lifted * mask * slope).astype(BF16)


def coarse_outputs(
    size_y, low_ref, mid_ref, high_ref, hidden_ref, grad_ref, lift_ref, up_ref, fine_ref,
    mask_ref, spread_ref, net_ref, grad_coarse_ref, grad_up_ref, cols_ref,
):
    chans = low_ref.shape[0]
    planes = mid_ref.shape[0] // chans
    inner = hidden_ref.shape[0] // planes
    depth = 9 * chans
    gather_planes(gather_coarse, low_ref, mid_ref, high_ref, chans, size_y // 2, cols_ref)
    lifted = dot(up_ref[...], hidden_ref[...])
    high, low = halves(lifted)
    wide = 4 * size_y
    for step in range(fine_ref.shape[1] // wide):
        lanes = slice(step * wide, (step + 1) * wide)
        coarse = slice(step * size_y, (step + 1) * size_y)
        spread = dot(high[:, coarse], spread_ref[...]) + dot(low[:, coarse], spread_ref[...])
        value = fine_ref[:, lanes].astype(F32) + mask_ref[:, lanes] * repeat_pairs(spread, chans)
        net_ref[:, lanes] = value.astype(BF16)
    lift_high, lift_low = halves(lift_ref[...])
    grad_coarse = 0.0
    grad_up = 0.0
    for x in range(planes):
        hidden = hidden_ref[x * inner : (x + 1) * inner, :]
        held = slice(x * chans, (x + 1) * chans)
        grad_up += dot_nt(lift_high[held], hidden) + dot_nt(lift_low[held], hidden)
        grad_coarse += dot_nt(
            cols_ref[x * depth : (x + 3) * depth, :], grad_ref[x * inner : (x + 1) * inner, :]
        )
    grad_coarse_ref[...] = grad_coarse
    grad_up_ref[...] = grad_up


def coarse_backward(
    size_y, low_ref, mid_ref, high_ref, taps_ref, cotangent_ref, slope_ref, spread_ref,
    grad_ref, cols_ref,
):
    inner = low_ref.shape[0]
    planes = mid_ref.shape[0] // inner
    chans = cotangent_ref.shape[0] // (2 * planes)
    gather_planes(gather_coarse, low_ref, mid_ref, high_ref, inner, size_y // 2, cols_ref)
    high, low = halves(dot(taps_ref[...], cols_ref[...]) * 0.125)
    wide = 4 * size_y
    for step in range(cotangent_ref.shape[1] // wide):
        lanes = slice(step * wide, (step + 1) * wide)
        coarse = slice(step * size_y, (step + 1) * size_y)
        spread = dot(high[:, coarse], spread_ref[...]) + dot(low[:, coarse], spread_ref[...])
        value = cotangent_ref[:, lanes].astype(F32) + repeat_pairs(spread, chans)
        grad_ref[:, lanes] = (value * slope_ref[:, lanes]).astype(BF16)


def fine_backward(
    size_y, low_ref, mid_ref, high_ref, taps_ref, features_ref,
    grad_features_ref, grad_fine_ref, cols_ref, framed_ref,
):
    chans = low_ref.shape[0]
    planes = mid_ref.shape[0] // chans
    length = mid_ref.shape[1]
    depth = 9 * chans
    gather_planes(gather_fine, low_ref, mid_ref, high_ref, chans, size_y, cols_ref)
    empty = jnp.zeros((2 * chans, length), BF16)
    framed_ref[: 2 * chans, :] = empty
    framed_ref[2 * chans : (planes + 2) * chans, :] = features_ref[...]
    framed_ref[(planes + 2) * chans :, :] = empty
    wide = 4 * size_y
    for group in range(planes // ALONG):
        rows = slice(group * ALONG * depth, (group * ALONG + ALONG + 2) * depth)
        held = slice(group * ALONG * chans, (group + 1) * ALONG * chans)
        for step in range(length // wide):
            lanes = slice(step * wide, (step + 1) * wide)
            grad_features_ref[held, lanes] = dot(taps_ref[...], cols_ref[rows, lanes])
    total = 0.0
    for plane in range(planes + 2):
        total += dot_nt(
            cols_ref[plane * depth : (plane + 1) * depth, :],
            framed_ref[plane * chans : (plane + 3) * chans, :],
        )
    grad_fine_ref[...] = total


def sum_over(
    count, chunk, factor, fine_ref, coarse_ref, up_ref, out_ref,
    packed, slots, part, whole, send_a, recv_a, send_b, recv_b,
):
    me = lax.axis_index("gx")
    barrier = pltpu.get_barrier_semaphore()

    def peer(d):
        return lax.rem(me + d, count)

    def greet(d, carry):
        pl.semaphore_signal(barrier, inc=1, device_id={"gx": peer(d)}, device_id_type=MESH)
        return carry

    lax.fori_loop(1, count, greet, 0)

    fine_rows, fine_cols = fine_ref.shape
    half = coarse_ref.shape[0] // 2
    coarse_cols = coarse_ref.shape[1]
    packed[...] = jnp.zeros(packed.shape, BF16)
    packed[:fine_rows, :fine_cols] = fine_ref[...].astype(BF16)
    packed[fine_rows : fine_rows + half, :coarse_cols] = coarse_ref[:half, :].astype(BF16)
    packed[fine_rows : fine_rows + half, coarse_cols : 2 * coarse_cols] = coarse_ref[
        half:, :
    ].astype(BF16)
    first = fine_rows + half
    packed[first : first + up_ref.shape[0], : up_ref.shape[1]] = up_ref[...].astype(BF16)
    pl.semaphore_wait(barrier, count - 1)

    def rows_of(index):
        return pl.ds(pl.multiple_of(index * chunk, chunk), chunk)

    def scatter(d):
        return pltpu.make_async_remote_copy(
            src_ref=packed.at[rows_of(peer(d))],
            dst_ref=slots.at[d],
            send_sem=send_a.at[d],
            recv_sem=recv_a.at[d],
            device_id={"gx": peer(d)},
            device_id_type=MESH,
        )

    def spread(d):
        return pltpu.make_async_remote_copy(
            src_ref=part,
            dst_ref=whole.at[rows_of(me)],
            send_sem=send_b.at[d],
            recv_sem=recv_b.at[d],
            device_id={"gx": peer(d)},
            device_id_type=MESH,
        )

    def start(copy):
        def body(d, carry):
            copy(d).start()
            return carry

        lax.fori_loop(1, count, body, 0)

    start(scatter)

    def add(d, total):
        scatter(d).wait_recv()
        return total + slots[d].astype(F32)

    total = lax.fori_loop(1, count, add, packed[rows_of(me), :].astype(F32))
    part[...] = (total * factor).astype(BF16)
    start(spread)
    whole[rows_of(me), :] = part[...]

    def finish(d, carry):
        scatter(d).wait_send()
        spread(d).wait_send()
        spread(d).wait_recv()
        return carry

    lax.fori_loop(1, count, finish, 0)
    out_ref[...] = whole[...].astype(F32)


def call(kernel, out_shape, scratch, *args, **params):
    flops = params.pop("flops", 0)
    size = sum(math.prod(a.shape) * a.dtype.itemsize for a in args)
    return pl.pallas_call(
        kernel,
        out_shape=out_shape,
        in_specs=[pl.BlockSpec(memory_space=pltpu.VMEM)] * len(args),
        out_specs=jax.tree.map(lambda _: pl.BlockSpec(memory_space=pltpu.VMEM), out_shape),
        scratch_shapes=scratch,
        compiler_params=pltpu.CompilerParams(vmem_limit_bytes=VMEM_LIMIT, **params),
        cost_estimate=pl.CostEstimate(flops=flops, bytes_accessed=2 * size, transcendentals=0),
    )(*args)


def banded(weight):
    outs, ins = weight.shape[:2]
    depth = 9 * ins
    taps = weight.transpose(0, 2, 3, 4, 1).reshape(outs, 3 * depth)
    return jnp.concatenate(
        [jnp.pad(taps, ((0, 0), (x * depth, (ALONG - 1 - x) * depth))) for x in range(ALONG)],
        axis=0,
    )


def flip_weight(weight):
    return jnp.flip(weight, (2, 3, 4)).transpose(1, 0, 2, 3, 4)


def planes_first(values):
    chans, size_x, size_z, size_y = values.shape
    return values.transpose(1, 0, 2, 3).reshape(size_x * chans, size_z * size_y)


def channels_first(values, chans, size_z, size_y):
    return values.reshape(-1, chans, size_z, size_y).transpose(1, 0, 2, 3)


def faces(values, chans):
    count = lax.axis_size("gx")
    forward = [(i, i + 1) for i in range(count - 1)]
    backward = [(target, source) for source, target in forward]
    low = lax.ppermute(values[-chans:], "gx", forward)
    high = lax.ppermute(values[:chans], "gx", backward)
    return low, values, high


def expand_row(blocks, times):
    values = blocks.astype(F32)[0]
    size_z, size_y = values.shape
    values = jnp.broadcast_to(values[:, None, :, None], (size_z, times, size_y, times))
    return values.reshape(1, size_z * times * size_y * times)


def per_device(features, active_blocks, weight_fine, weight_coarse, weight_up, cotangent):
    chans, size_x, size_z, size_y = features.shape
    inner = weight_coarse.shape[0]
    count = lax.axis_size("gx")
    factor = 1.0 / math.sqrt(size_x * count * size_z * size_y)
    length = size_z * size_y
    half_x, coarse_length = size_x // 2, length // 4
    shape = jax.ShapeDtypeStruct

    fine_mask = expand_row(active_blocks, 8)
    coarse_mask = expand_row(active_blocks, 4)
    pool = jnp.asarray(pool_matrix(size_y), BF16)
    spread = jnp.asarray(pool_matrix(size_y).T, BF16)
    diagonal = jnp.eye(half_x, dtype=BF16)
    up_blocks = jnp.kron(diagonal, weight_up)
    back_blocks = jnp.kron(diagonal, weight_up.T)

    rows = planes_first(features)
    fine_faces = faces(rows, chans)
    cotangent_rows = planes_first(cotangent)

    fine_cols = pltpu.VMEM(((size_x + 2) * 9 * chans, length), BF16)
    hidden_fine, slope_fine, pooled = call(
        functools.partial(fine_forward, size_y),
        (
            shape((size_x * chans, length), BF16),
            shape((size_x * chans, length), F32),
            shape((half_x * chans, coarse_length), BF16),
        ),
        [fine_cols],
        *fine_faces, banded(weight_fine), fine_mask, pool,
    )
    pooled_faces = faces(pooled, chans)
    grad_lift = call(
        functools.partial(lift_pool, size_y, chans),
        shape((half_x * chans, coarse_length), F32),
        [],
        cotangent_rows, fine_mask, pool,
    )
    coarse_cols = pltpu.VMEM(((half_x + 2) * 9 * chans, coarse_length), BF16)
    hidden_coarse, grad_pre_coarse = call(
        functools.partial(coarse_forward, size_y // 2),
        (
            shape((half_x * inner, coarse_length), BF16),
            shape((half_x * inner, coarse_length), BF16),
        ),
        [coarse_cols],
        *pooled_faces, banded(weight_coarse), coarse_mask, grad_lift, back_blocks,
    )
    grad_faces = faces(grad_pre_coarse, inner)
    net_rows, grad_coarse, grad_up = call(
        functools.partial(coarse_outputs, size_y),
        (
            shape((size_x * chans, length), BF16),
            shape((27 * chans, inner), F32),
            shape((chans, inner), F32),
        ),
        [coarse_cols],
        *pooled_faces, hidden_coarse, grad_pre_coarse, grad_lift, up_blocks, hidden_fine,
        fine_mask, spread,
    )
    grad_pre_fine = call(
        functools.partial(coarse_backward, size_y),
        shape((size_x * chans, length), BF16),
        [pltpu.VMEM(((half_x + 2) * 9 * inner, coarse_length), BF16)],
        *grad_faces, banded(flip_weight(weight_coarse)), cotangent_rows, slope_fine, spread,
    )
    grad_fine_faces = faces(grad_pre_fine, chans)
    net_output = channels_first(net_rows, chans, size_z, size_y)
    grad_rows, grad_fine = call(
        functools.partial(fine_backward, size_y),
        (shape((size_x * chans, length), F32), shape((9 * chans, 3 * chans), F32)),
        [fine_cols, pltpu.VMEM(((size_x + 4) * chans, length), BF16)],
        *grad_fine_faces, banded(flip_weight(weight_fine)), rows,
    )
    used = 9 * chans + (27 * chans + 1) // 2 + chans
    chunk = -(-used // (16 * count)) * 16
    lanes = max(2 * inner, 3 * chans)
    sums = call(
        functools.partial(sum_over, count, chunk, factor),
        shape((count * chunk, lanes), F32),
        [
            pltpu.VMEM((count * chunk, lanes), BF16),
            pltpu.VMEM((count, chunk, lanes), BF16),
            pltpu.VMEM((chunk, lanes), BF16),
            pltpu.VMEM((count * chunk, lanes), BF16),
            pltpu.SemaphoreType.DMA((count,)),
            pltpu.SemaphoreType.DMA((count,)),
            pltpu.SemaphoreType.DMA((count,)),
            pltpu.SemaphoreType.DMA((count,)),
        ],
        grad_fine, grad_coarse, grad_up,
        collective_id=0, has_side_effects=True,
    )
    grad_features = channels_first(grad_rows, chans, size_z, size_y)
    fine_rows, half = 9 * chans, 27 * chans // 2
    grad_fine = sums[:fine_rows, : 3 * chans].reshape(3, 3, chans, 3, chans)
    grad_fine = jnp.flip(grad_fine, (0, 1)).transpose(2, 4, 3, 0, 1)
    grad_coarse = sums[fine_rows : fine_rows + half, : 2 * inner]
    grad_coarse = jnp.concatenate([grad_coarse[:, :inner], grad_coarse[:, inner:]], axis=0)
    grad_coarse = grad_coarse.reshape(3, 3, 3, chans, inner).transpose(4, 3, 0, 1, 2)
    grad_up = sums[fine_rows + half : fine_rows + half + chans, :inner]
    return (net_output, grad_features, grad_fine, grad_coarse, grad_up)


def solution(mesh):
    return jax.shard_map(
        per_device,
        mesh=mesh,
        in_specs=(
            P(None, ("groups", "gx"), None, None),
            P(("groups", "gx"), None, None),
            P(),
            P(),
            P(),
            P(None, ("groups", "gx"), None, None),
        ),
        out_specs=(
            P(None, ("groups", "gx"), None, None),
            P(None, ("groups", "gx"), None, None),
            P("groups", None, None, None, None),
            P("groups", None, None, None, None),
            P("groups", None),
        ),
        check_vma=False,
    )
```

```python
import functools
import math

import jax
import jax.numpy as jnp
import numpy as np
from jax import lax
from jax.experimental import pallas as pl
from jax.experimental.pallas import tpu as pltpu
from jax.sharding import PartitionSpec as P

F32 = jnp.float32
BF16 = jnp.bfloat16
VMEM_LIMIT = 48 * 1024 * 1024
MESH = pl.DeviceIdType.MESH
ALONG = 4


def dot(a, b):
    return jnp.dot(a, b, preferred_element_type=F32)


def dot_nt(a, b):
    return lax.dot_general(a, b, (((1,), (1,)), ((), ())), preferred_element_type=F32)


def dot_tn(a, b):
    return lax.dot_general(a, b, (((0,), (0,)), ((), ())), preferred_element_type=F32)


def halves(value):
    high = value.astype(BF16)
    return high, (value - high.astype(F32)).astype(BF16)


def pool_matrix(size_y):
    cell = np.arange(4 * size_y)
    coarse = np.arange(size_y)
    same_z = (cell // size_y // 2)[:, None] == (coarse // (size_y // 2))[None]
    same_y = (cell % size_y // 2)[:, None] == (coarse % (size_y // 2))[None]
    return (same_z & same_y).astype(np.float32)


def gather_fine(value, size_y, cols_ref, row, reverse):
    chans, length = value.shape
    wide = value.astype(F32)
    spot = lax.broadcasted_iota(jnp.int32, (chans, length), 1) % size_y
    before = jnp.where(spot == 0, 0.0, pltpu.roll(wide, 1, 1)).astype(BF16)
    after = jnp.where(spot == size_y - 1, 0.0, pltpu.roll(wide, length - 1, 1)).astype(BF16)
    edge = jnp.zeros((chans, size_y), BF16)
    blocks = (after, value, before) if reverse else (before, value, after)
    for k, shifted in enumerate(blocks):
        low = pl.ds(row + (k + (6 if reverse else 0)) * chans, chans)
        mid = pl.ds(row + (3 + k) * chans, chans)
        high = pl.ds(row + (k + (0 if reverse else 6)) * chans, chans)
        cols_ref[low, :size_y] = edge
        cols_ref[low, size_y:] = shifted[:, :-size_y]
        cols_ref[mid, :] = shifted
        cols_ref[high, : length - size_y] = shifted[:, size_y:]
        cols_ref[high, length - size_y :] = edge


def gather_coarse(value, size_y, cols_ref, row, reverse):
    chans, length = value.shape
    wide = value.astype(F32)
    cell = lax.broadcasted_iota(jnp.int32, (chans, length), 1)
    spot = cell % size_y
    for j in range(3):
        for k in range(3):
            shift = (j - 1) * size_y + (k - 1)
            rolled = pltpu.roll(wide, (-shift) % length, 1) if shift else wide
            if k == 0:
                rolled = jnp.where(spot == 0, 0.0, rolled)
            if k == 2:
                rolled = jnp.where(spot == size_y - 1, 0.0, rolled)
            if j == 0:
                rolled = jnp.where(cell < size_y, 0.0, rolled)
            if j == 2:
                rolled = jnp.where(cell >= length - size_y, 0.0, rolled)
            tap = 3 * j + k
            block = 8 - tap if reverse else tap
            cols_ref[pl.ds(row + block * chans, chans), :] = rolled.astype(BF16)


def gather_inner(gather, mid_ref, chans, size_y, cols_ref, reverse):
    depth = 9 * chans

    def body(plane, carry):
        start = pl.multiple_of(plane * chans, chans)
        row = pl.multiple_of((plane + 1) * depth, depth)
        gather(mid_ref[pl.ds(start, chans), :], size_y, cols_ref, row, reverse)
        return carry

    lax.fori_loop(0, mid_ref.shape[0] // chans, body, 0)


def gather_edges(gather, edge_ref, size_y, cols_ref, reverse):
    last = cols_ref.shape[0] - 9 * edge_ref.shape[1]
    gather(edge_ref[0], size_y, cols_ref, 0, reverse)
    gather(edge_ref[1], size_y, cols_ref, last, reverse)


def sum_pairs(value, chans):
    count = value.shape[0] // chans
    return jnp.concatenate(
        [
            value[(2 * i) * chans : (2 * i + 1) * chans]
            + value[(2 * i + 1) * chans : (2 * i + 2) * chans]
            for i in range(count // 2)
        ],
        axis=0,
    )


def repeat_pairs(value, chans):
    count = value.shape[0] // chans
    parts = [value[i // 2 * chans : (i // 2 + 1) * chans] for i in range(2 * count)]
    return jnp.concatenate(parts, axis=0)


def sigmoid(value):
    return 1.0 / (1.0 + jnp.exp(-value))


def whole_step(
    count, chunk, factor, size_y,
    rows_ref, cotangent_ref, fine_mask_ref, coarse_mask_ref, pool_ref, spread_ref,
    fine_taps_ref, coarse_taps_ref, coarse_back_ref, fine_back_ref, up_ref,
    net_ref, grad_rows_ref, grad_fine_ref, grad_coarse_ref, grad_up_ref,
    fine_cols, coarse_cols, inner_cols, hidden_ref, slope_ref, pooled_ref, inner_ref, grad_inner_ref,
    grad_pre_ref, lift_ref, framed, fine_edge, pooled_edge, inner_edge, grad_edge,
    packed, slots, part, whole,
    send_low, recv_low, send_high, recv_high, send_a, recv_a, send_b, recv_b,
):
    me = lax.axis_index("gx")
    out_chans, inner = up_ref.shape
    chans = out_chans
    planes = rows_ref.shape[0] // chans
    half = planes // 2
    length = rows_ref.shape[1]
    depth = 9 * chans
    wide = 4 * size_y
    steps = length // wide
    half_y = size_y // 2
    barrier = pltpu.get_barrier_semaphore()

    def peer(d):
        return lax.rem(me + d, count)

    def greet(d, carry):
        pl.semaphore_signal(barrier, inc=1, device_id={"gx": peer(d)}, device_id_type=MESH)
        return carry

    lax.fori_loop(1, count, greet, 0)

    def upward(index, values_ref, edge_ref):
        size = edge_ref.shape[1]
        return pltpu.make_async_remote_copy(
            src_ref=values_ref.at[pl.ds(values_ref.shape[0] - size, size)],
            dst_ref=edge_ref.at[0],
            send_sem=send_low.at[index],
            recv_sem=recv_low.at[index],
            device_id={"gx": lax.rem(me + 1, count)},
            device_id_type=MESH,
        )

    def downward(index, values_ref, edge_ref):
        size = edge_ref.shape[1]
        return pltpu.make_async_remote_copy(
            src_ref=values_ref.at[pl.ds(0, size)],
            dst_ref=edge_ref.at[1],
            send_sem=send_high.at[index],
            recv_sem=recv_high.at[index],
            device_id={"gx": lax.rem(me + count - 1, count)},
            device_id_type=MESH,
        )

    def start_upward(*args):
        @pl.when(me < count - 1)
        def _():
            upward(*args).start()

    def start_downward(*args):
        @pl.when(me > 0)
        def _():
            downward(*args).start()

    def finish_edges(*args):
        edge_ref = args[2]

        @pl.when(me > 0)
        def _():
            upward(*args).wait_recv()
            downward(*args).wait_send()

        @pl.when(me == 0)
        def _():
            edge_ref[0] = jnp.zeros(edge_ref.shape[1:], BF16)

        @pl.when(me < count - 1)
        def _():
            downward(*args).wait_recv()
            upward(*args).wait_send()

        @pl.when(me == count - 1)
        def _():
            edge_ref[1] = jnp.zeros(edge_ref.shape[1:], BF16)

    for step in range(steps):
        lanes = slice(step * wide, (step + 1) * wide)
        value = (cotangent_ref[:, lanes].astype(F32) * fine_mask_ref[:, lanes]).astype(BF16)
        lift_ref[:, step * size_y : (step + 1) * size_y] = sum_pairs(
            dot(value, pool_ref[...]), chans
        )
    empty = jnp.zeros((2 * chans, length), BF16)
    framed[: 2 * chans, :] = empty
    framed[2 * chans : (planes + 2) * chans, :] = rows_ref[...]
    framed[(planes + 2) * chans :, :] = empty

    pl.semaphore_wait(barrier, count - 1)
    start_upward(0, rows_ref, fine_edge)
    start_downward(0, rows_ref, fine_edge)
    gather_inner(gather_fine, rows_ref, chans, size_y, fine_cols, False)
    finish_edges(0, rows_ref, fine_edge)
    gather_edges(gather_fine, fine_edge, size_y, fine_cols, False)
    for group in range(planes // ALONG):
        rows = slice(group * ALONG * depth, (group * ALONG + ALONG + 2) * depth)
        held = slice(group * ALONG * chans, (group + 1) * ALONG * chans)
        out = slice(group * ALONG // 2 * chans, (group + 1) * ALONG // 2 * chans)
        for step in range(steps):
            lanes = slice(step * wide, (step + 1) * wide)
            pre = dot(fine_taps_ref[...], fine_cols[rows, lanes])
            mask = fine_mask_ref[:, lanes]
            sigma = sigmoid(pre)
            hidden = (pre * sigma * mask).astype(BF16)
            hidden_ref[held, lanes] = hidden
            slope_ref[held, lanes] = sigma * (1.0 + pre * (1.0 - sigma)) * mask
            pooled = sum_pairs(dot(hidden, pool_ref[...]), chans) * 0.125
            pooled_ref[out, step * size_y : (step + 1) * size_y] = pooled.astype(BF16)
        if group == 0:
            start_downward(1, pooled_ref, pooled_edge)
    start_upward(1, pooled_ref, pooled_edge)

    gather_inner(gather_coarse, pooled_ref, chans, half_y, coarse_cols, False)
    lift_high, lift_low = halves(lift_ref[...])
    up = up_ref[...]
    lifted_grads = []
    for x in range(half):
        held = slice(x * chans, (x + 1) * chans)
        lifted_grads.append(dot_tn(up, lift_high[held]) + dot_tn(up, lift_low[held]))
    grad_hidden = jnp.concatenate(lifted_grads, axis=0)
    finish_edges(1, pooled_ref, pooled_edge)
    gather_edges(gather_coarse, pooled_edge, half_y, coarse_cols, False)
    pre = dot(coarse_taps_ref[...], coarse_cols[...])
    mask = coarse_mask_ref[...]
    sigma = sigmoid(pre)
    slope = sigma * (1.0 + pre * (1.0 - sigma))
    grad_inner_ref[...] = (grad_hidden * mask * slope).astype(BF16)
    start_downward(2, grad_inner_ref, inner_edge)
    start_upward(2, grad_inner_ref, inner_edge)
    inner_ref[...] = (pre * sigma * mask).astype(BF16)
    gather_inner(gather_coarse, grad_inner_ref, inner, half_y, inner_cols, True)

    lifted = jnp.concatenate(
        [dot(up, inner_ref[x * inner : (x + 1) * inner, :]) for x in range(half)], axis=0
    )
    high, low = halves(lifted)
    for step in range(steps):
        lanes = slice(step * wide, (step + 1) * wide)
        coarse = slice(step * size_y, (step + 1) * size_y)
        spread = dot(high[:, coarse], spread_ref[...]) + dot(low[:, coarse], spread_ref[...])
        value = hidden_ref[:, lanes].astype(F32) + fine_mask_ref[:, lanes] * repeat_pairs(
            spread, chans
        )
        net_ref[:, lanes] = value.astype(BF16)
    grad_coarse = 0.0
    grad_up = 0.0
    for x in range(half):
        hidden = inner_ref[x * inner : (x + 1) * inner, :]
        held = slice(x * chans, (x + 1) * chans)
        grad_up += dot_nt(lift_high[held], hidden) + dot_nt(lift_low[held], hidden)
        grad_coarse += dot_nt(
            coarse_cols[x * depth : (x + 3) * depth, :],
            grad_inner_ref[x * inner : (x + 1) * inner, :],
        )
    split = 3 * depth // 2
    packed[depth + split + chans :, :] = jnp.zeros(
        (packed.shape[0] - depth - split - chans, packed.shape[1]), BF16
    )
    packed[depth : depth + split, :] = jnp.concatenate(
        [grad_coarse[:split], grad_coarse[split:]], axis=1
    ).astype(BF16)
    packed[depth + split : depth + split + chans, :] = jnp.concatenate(
        [grad_up, jnp.zeros_like(grad_up)], axis=1
    ).astype(BF16)

    finish_edges(2, grad_inner_ref, inner_edge)
    gather_edges(gather_coarse, inner_edge, half_y, inner_cols, True)
    high, low = halves(dot(coarse_back_ref[...], inner_cols[...]) * 0.125)
    for step in range(steps):
        lanes = slice(step * wide, (step + 1) * wide)
        coarse = slice(step * size_y, (step + 1) * size_y)
        spread = dot(high[:, coarse], spread_ref[...]) + dot(low[:, coarse], spread_ref[...])
        value = cotangent_ref[:, lanes].astype(F32) + repeat_pairs(spread, chans)
        grad_pre_ref[:, lanes] = (value * slope_ref[:, lanes]).astype(BF16)
    start_downward(3, grad_pre_ref, grad_edge)
    start_upward(3, grad_pre_ref, grad_edge)

    gather_inner(gather_fine, grad_pre_ref, chans, size_y, fine_cols, True)

    def taps_of(plane):
        return dot_nt(
            fine_cols[plane * depth : (plane + 1) * depth, :],
            framed[plane * chans : (plane + 3) * chans, :],
        )

    grad_fine = 0.0
    for plane in range(1, planes + 1):
        grad_fine += taps_of(plane)
    finish_edges(3, grad_pre_ref, grad_edge)
    gather_edges(gather_fine, grad_edge, size_y, fine_cols, True)
    grad_fine += taps_of(0) + taps_of(planes + 1)
    fill = packed.shape[1] - grad_fine.shape[1]
    packed[:depth, :] = jnp.concatenate(
        [grad_fine, jnp.zeros((depth, fill), F32)], axis=1
    ).astype(BF16)

    def rows_of(index):
        return pl.ds(pl.multiple_of(index * chunk, chunk), chunk)

    def scatter(d):
        return pltpu.make_async_remote_copy(
            src_ref=packed.at[rows_of(peer(d))],
            dst_ref=slots.at[d],
            send_sem=send_a.at[d],
            recv_sem=recv_a.at[d],
            device_id={"gx": peer(d)},
            device_id_type=MESH,
        )

    def collect(d):
        return pltpu.make_async_remote_copy(
            src_ref=part,
            dst_ref=whole.at[rows_of(me)],
            send_sem=send_b.at[d],
            recv_sem=recv_b.at[d],
            device_id={"gx": peer(d)},
            device_id_type=MESH,
        )

    def start(copy):
        def body(d, carry):
            copy(d).start()
            return carry

        lax.fori_loop(1, count, body, 0)

    def features_grad(group):
        rows = slice(group * ALONG * depth, (group * ALONG + ALONG + 2) * depth)
        held = slice(group * ALONG * chans, (group + 1) * ALONG * chans)
        for step in range(steps):
            lanes = slice(step * wide, (step + 1) * wide)
            grad_rows_ref[held, lanes] = dot(fine_back_ref[...], fine_cols[rows, lanes])

    start(scatter)
    groups = planes // ALONG
    for group in range(groups // 2):
        features_grad(group)

    def add(d, total):
        scatter(d).wait_recv()
        return total + slots[d].astype(F32)

    total = lax.fori_loop(1, count, add, packed[rows_of(me), :].astype(F32))
    part[...] = (total * factor).astype(BF16)
    start(collect)
    whole[rows_of(me), :] = part[...]
    for group in range(groups // 2, groups):
        features_grad(group)

    def finish(d, carry):
        scatter(d).wait_send()
        collect(d).wait_send()
        collect(d).wait_recv()
        return carry

    lax.fori_loop(1, count, finish, 0)
    sums = whole[...].astype(F32)
    for i in range(3):
        grad_fine_ref[i * depth : (i + 1) * depth, :] = sums[:depth, i * chans : (i + 1) * chans]
    grad_coarse_ref[:split, :] = sums[depth : depth + split, :inner]
    grad_coarse_ref[split:, :] = sums[depth : depth + split, inner : 2 * inner]
    grad_up_ref[...] = sums[depth + split : depth + split + chans, :inner]


def banded(taps, reverse):
    outs, _, depth = taps.shape
    parts = [taps[:, i] for i in (range(2, -1, -1) if reverse else range(3))]
    flat = jnp.concatenate(parts, axis=1)
    return jnp.concatenate(
        [jnp.pad(flat, ((0, 0), (x * depth, (ALONG - 1 - x) * depth))) for x in range(ALONG)],
        axis=0,
    )


def forward_taps(weight):
    outs, ins = weight.shape[:2]
    return banded(weight.transpose(0, 2, 3, 4, 1).reshape(outs, 3, 9 * ins), False)


def backward_taps(weight):
    outs, ins = weight.shape[:2]
    return banded(weight.transpose(1, 2, 3, 4, 0).reshape(ins, 3, 9 * outs), True)


def planes_first(values):
    chans, size_x, size_z, size_y = values.shape
    return values.transpose(1, 0, 2, 3).reshape(size_x * chans, size_z * size_y)


def channels_first(values, chans, size_z, size_y):
    return values.reshape(-1, chans, size_z, size_y).transpose(1, 0, 2, 3)


def expand_row(blocks, times):
    values = blocks.astype(F32)[0]
    size_z, size_y = values.shape
    values = jnp.broadcast_to(values[:, None, :, None], (size_z, times, size_y, times))
    return values.reshape(1, size_z * times * size_y * times)


def per_device(features, active_blocks, weight_fine, weight_coarse, weight_up, cotangent):
    chans, size_x, size_z, size_y = features.shape
    inner = weight_coarse.shape[0]
    count = lax.axis_size("gx")
    factor = 1.0 / math.sqrt(size_x * count * size_z * size_y)
    length = size_z * size_y
    half_x, coarse_length = size_x // 2, length // 4
    used = 9 * chans + (27 * chans) // 2 + chans
    chunk = -(-used // (16 * count)) * 16
    lanes = 2 * inner
    shape = jax.ShapeDtypeStruct
    args = (
        planes_first(features),
        planes_first(cotangent),
        expand_row(active_blocks, 8),
        expand_row(active_blocks, 4),
        jnp.asarray(pool_matrix(size_y), BF16),
        jnp.asarray(pool_matrix(size_y).T, BF16),
        forward_taps(weight_fine),
        forward_taps(weight_coarse),
        backward_taps(weight_coarse),
        backward_taps(weight_fine),
        weight_up,
    )
    out_shape = (
        shape((size_x * chans, length), BF16),
        shape((size_x * chans, length), F32),
        shape((27 * chans, chans), F32),
        shape((27 * chans, inner), F32),
        shape((chans, inner), F32),
    )
    scratch = [
        pltpu.VMEM(((size_x + 2) * 9 * chans, length), BF16),
        pltpu.VMEM(((half_x + 2) * 9 * chans, coarse_length), BF16),
        pltpu.VMEM(((half_x + 2) * 9 * inner, coarse_length), BF16),
        pltpu.VMEM((size_x * chans, length), BF16),
        pltpu.VMEM((size_x * chans, length), F32),
        pltpu.VMEM((half_x * chans, coarse_length), BF16),
        pltpu.VMEM((half_x * inner, coarse_length), BF16),
        pltpu.VMEM((half_x * inner, coarse_length), BF16),
        pltpu.VMEM((size_x * chans, length), BF16),
        pltpu.VMEM((half_x * chans, coarse_length), F32),
        pltpu.VMEM(((size_x + 4) * chans, length), BF16),
        pltpu.VMEM((2, chans, length), BF16),
        pltpu.VMEM((2, chans, coarse_length), BF16),
        pltpu.VMEM((2, inner, coarse_length), BF16),
        pltpu.VMEM((2, chans, length), BF16),
        pltpu.VMEM((count * chunk, lanes), BF16),
        pltpu.VMEM((count, chunk, lanes), BF16),
        pltpu.VMEM((chunk, lanes), BF16),
        pltpu.VMEM((count * chunk, lanes), BF16),
    ]
    scratch += [pltpu.SemaphoreType.DMA((4,))] * 4 + [pltpu.SemaphoreType.DMA((count,))] * 4
    net_rows, grad_rows, grad_fine, grad_coarse, grad_up = pl.pallas_call(
        functools.partial(whole_step, count, chunk, factor, size_y),
        out_shape=out_shape,
        in_specs=[pl.BlockSpec(memory_space=pltpu.VMEM)] * len(args),
        out_specs=tuple(pl.BlockSpec(memory_space=pltpu.VMEM) for _ in out_shape),
        scratch_shapes=scratch,
        compiler_params=pltpu.CompilerParams(
            vmem_limit_bytes=VMEM_LIMIT, collective_id=0, has_side_effects=True
        ),
    )(*args)
    taps = (3, 3, 3)
    return (
        channels_first(net_rows, chans, size_z, size_y),
        channels_first(grad_rows, chans, size_z, size_y),
        grad_fine.reshape(taps + (chans, chans)).transpose(3, 4, 0, 1, 2),
        grad_coarse.reshape(taps + (chans, inner)).transpose(4, 3, 0, 1, 2),
        grad_up,
    )


def solution(mesh):
    return jax.shard_map(
        per_device,
        mesh=mesh,
        in_specs=(
            P(None, ("groups", "gx"), None, None),
            P(("groups", "gx"), None, None),
            P(),
            P(),
            P(),
            P(None, ("groups", "gx"), None, None),
        ),
        out_specs=(
            P(None, ("groups", "gx"), None, None),
            P(None, ("groups", "gx"), None, None),
            P("groups", None, None, None, None),
            P("groups", None, None, None, None),
            P("groups", None),
        ),
        check_vma=False,
    )
```

```python
import functools
import math

import jax
import jax.numpy as jnp
import numpy as np
from jax import lax
from jax.experimental import pallas as pl
from jax.experimental.pallas import tpu as pltpu
from jax.sharding import PartitionSpec as P

F32 = jnp.float32
BF16 = jnp.bfloat16
VMEM_LIMIT = 48 * 1024 * 1024
MESH = pl.DeviceIdType.MESH
ALONG = 4


def dot(a, b):
    return jnp.dot(a, b, preferred_element_type=F32)


def dot_nt(a, b):
    return lax.dot_general(a, b, (((1,), (1,)), ((), ())), preferred_element_type=F32)


def dot_tn(a, b):
    return lax.dot_general(a, b, (((0,), (0,)), ((), ())), preferred_element_type=F32)


def halves(value):
    high = value.astype(BF16)
    return high, (value - high.astype(F32)).astype(BF16)


def pool_matrix(size_y):
    cell = np.arange(4 * size_y)
    coarse = np.arange(size_y)
    same_z = (cell // size_y // 2)[:, None] == (coarse // (size_y // 2))[None]
    same_y = (cell % size_y // 2)[:, None] == (coarse % (size_y // 2))[None]
    return (same_z & same_y).astype(np.float32)


def gather_fine(value, size_y, cols_ref, row, reverse):
    chans, length = value.shape
    wide = value.astype(F32)
    spot = lax.broadcasted_iota(jnp.int32, (chans, length), 1) % size_y
    before = jnp.where(spot == 0, 0.0, pltpu.roll(wide, 1, 1)).astype(BF16)
    after = jnp.where(spot == size_y - 1, 0.0, pltpu.roll(wide, length - 1, 1)).astype(BF16)
    edge = jnp.zeros((chans, size_y), BF16)
    blocks = (after, value, before) if reverse else (before, value, after)
    for k, shifted in enumerate(blocks):
        low = pl.ds(row + (k + (6 if reverse else 0)) * chans, chans)
        mid = pl.ds(row + (3 + k) * chans, chans)
        high = pl.ds(row + (k + (0 if reverse else 6)) * chans, chans)
        cols_ref[low, :size_y] = edge
        cols_ref[low, size_y:] = shifted[:, :-size_y]
        cols_ref[mid, :] = shifted
        cols_ref[high, : length - size_y] = shifted[:, size_y:]
        cols_ref[high, length - size_y :] = edge


def gather_coarse(value, size_y, cols_ref, row, reverse):
    chans, length = value.shape
    wide = value.astype(F32)
    cell = lax.broadcasted_iota(jnp.int32, (chans, length), 1)
    spot = cell % size_y
    for j in range(3):
        for k in range(3):
            shift = (j - 1) * size_y + (k - 1)
            rolled = pltpu.roll(wide, (-shift) % length, 1) if shift else wide
            if k == 0:
                rolled = jnp.where(spot == 0, 0.0, rolled)
            if k == 2:
                rolled = jnp.where(spot == size_y - 1, 0.0, rolled)
            if j == 0:
                rolled = jnp.where(cell < size_y, 0.0, rolled)
            if j == 2:
                rolled = jnp.where(cell >= length - size_y, 0.0, rolled)
            tap = 3 * j + k
            block = 8 - tap if reverse else tap
            cols_ref[pl.ds(row + block * chans, chans), :] = rolled.astype(BF16)


def gather_inner(gather, mid_ref, chans, size_y, cols_ref, reverse):
    depth = 9 * chans

    def body(plane, carry):
        start = pl.multiple_of(plane * chans, chans)
        row = pl.multiple_of((plane + 1) * depth, depth)
        gather(mid_ref[pl.ds(start, chans), :], size_y, cols_ref, row, reverse)
        return carry

    lax.fori_loop(0, mid_ref.shape[0] // chans, body, 0)


def gather_edges(gather, edge_ref, size_y, cols_ref, reverse):
    last = cols_ref.shape[0] - 9 * edge_ref.shape[1]
    gather(edge_ref[0], size_y, cols_ref, 0, reverse)
    gather(edge_ref[1], size_y, cols_ref, last, reverse)


def sum_pairs(value, chans):
    count = value.shape[0] // chans
    return jnp.concatenate(
        [
            value[(2 * i) * chans : (2 * i + 1) * chans]
            + value[(2 * i + 1) * chans : (2 * i + 2) * chans]
            for i in range(count // 2)
        ],
        axis=0,
    )


def repeat_pairs(value, chans):
    count = value.shape[0] // chans
    parts = [value[i // 2 * chans : (i // 2 + 1) * chans] for i in range(2 * count)]
    return jnp.concatenate(parts, axis=0)


def sigmoid(value):
    return 1.0 / (1.0 + jnp.exp(-value))


def whole_step(
    count, factor, size_y,
    rows_ref, cotangent_ref, fine_mask_ref, coarse_mask_ref, pool_ref, spread_ref,
    fine_taps_ref, coarse_taps_ref, coarse_back_ref, fine_back_ref, up_ref,
    net_ref, grad_rows_ref, grad_fine_ref, grad_coarse_ref, grad_up_ref,
    fine_cols, coarse_cols, inner_cols, hidden_ref, slope_ref, pooled_ref, inner_ref, grad_inner_ref,
    grad_pre_ref, lift_ref, framed, fine_edge, pooled_edge, inner_edge, grad_edge,
    inner_sum, fine_sum,
    send_low, recv_low, send_high, recv_high,
):
    me = lax.axis_index("gx")
    out_chans, inner = up_ref.shape
    chans = out_chans
    planes = rows_ref.shape[0] // chans
    half = planes // 2
    length = rows_ref.shape[1]
    depth = 9 * chans
    wide = 4 * size_y
    steps = length // wide
    half_y = size_y // 2
    barrier = pltpu.get_barrier_semaphore()

    def peer(d):
        return lax.rem(me + d, count)

    def greet(d, carry):
        pl.semaphore_signal(barrier, inc=1, device_id={"gx": peer(d)}, device_id_type=MESH)
        return carry

    lax.fori_loop(1, count, greet, 0)

    def scatter(refs, d):
        packed, slots, _, _, send, recv, _, _ = refs
        chunk = slots.shape[1]
        return pltpu.make_async_remote_copy(
            src_ref=packed.at[pl.ds(pl.multiple_of(peer(d) * chunk, chunk), chunk)],
            dst_ref=slots.at[d],
            send_sem=send.at[d],
            recv_sem=recv.at[d],
            device_id={"gx": peer(d)},
            device_id_type=MESH,
        )

    def collect(refs, d):
        _, _, part, whole, _, _, send, recv = refs
        chunk = part.shape[0]
        return pltpu.make_async_remote_copy(
            src_ref=part,
            dst_ref=whole.at[pl.ds(pl.multiple_of(me * chunk, chunk), chunk)],
            send_sem=send.at[d],
            recv_sem=recv.at[d],
            device_id={"gx": peer(d)},
            device_id_type=MESH,
        )

    def start(copy, refs):
        def body(d, carry):
            copy(refs, d).start()
            return carry

        lax.fori_loop(1, count, body, 0)

    def add_up(refs):
        packed, slots, part, whole = refs[:4]
        chunk = part.shape[0]
        mine = pl.ds(pl.multiple_of(me * chunk, chunk), chunk)

        def add(d, total):
            scatter(refs, d).wait_recv()
            return total + slots[d].astype(F32)

        total = lax.fori_loop(1, count, add, packed[mine, :].astype(F32))
        part[...] = (total * factor).astype(BF16)
        start(collect, refs)
        whole[mine, :] = part[...]

    def finish(refs):
        def body(d, carry):
            scatter(refs, d).wait_send()
            collect(refs, d).wait_send()
            collect(refs, d).wait_recv()
            return carry

        lax.fori_loop(1, count, body, 0)
        return refs[3][...].astype(F32)

    def upward(index, values_ref, edge_ref):
        size = edge_ref.shape[1]
        return pltpu.make_async_remote_copy(
            src_ref=values_ref.at[pl.ds(values_ref.shape[0] - size, size)],
            dst_ref=edge_ref.at[0],
            send_sem=send_low.at[index],
            recv_sem=recv_low.at[index],
            device_id={"gx": lax.rem(me + 1, count)},
            device_id_type=MESH,
        )

    def downward(index, values_ref, edge_ref):
        size = edge_ref.shape[1]
        return pltpu.make_async_remote_copy(
            src_ref=values_ref.at[pl.ds(0, size)],
            dst_ref=edge_ref.at[1],
            send_sem=send_high.at[index],
            recv_sem=recv_high.at[index],
            device_id={"gx": lax.rem(me + count - 1, count)},
            device_id_type=MESH,
        )

    def start_upward(*args):
        @pl.when(me < count - 1)
        def _():
            upward(*args).start()

    def start_downward(*args):
        @pl.when(me > 0)
        def _():
            downward(*args).start()

    def finish_edges(*args):
        edge_ref = args[2]

        @pl.when(me > 0)
        def _():
            upward(*args).wait_recv()
            downward(*args).wait_send()

        @pl.when(me == 0)
        def _():
            edge_ref[0] = jnp.zeros(edge_ref.shape[1:], BF16)

        @pl.when(me < count - 1)
        def _():
            downward(*args).wait_recv()
            upward(*args).wait_send()

        @pl.when(me == count - 1)
        def _():
            edge_ref[1] = jnp.zeros(edge_ref.shape[1:], BF16)

    for step in range(steps):
        lanes = slice(step * wide, (step + 1) * wide)
        value = (cotangent_ref[:, lanes].astype(F32) * fine_mask_ref[:, lanes]).astype(BF16)
        lift_ref[:, step * size_y : (step + 1) * size_y] = sum_pairs(
            dot(value, pool_ref[...]), chans
        )
    empty = jnp.zeros((2 * chans, length), BF16)
    framed[: 2 * chans, :] = empty
    framed[2 * chans : (planes + 2) * chans, :] = rows_ref[...]
    framed[(planes + 2) * chans :, :] = empty

    pl.semaphore_wait(barrier, count - 1)
    start_upward(0, rows_ref, fine_edge)
    start_downward(0, rows_ref, fine_edge)
    gather_inner(gather_fine, rows_ref, chans, size_y, fine_cols, False)
    finish_edges(0, rows_ref, fine_edge)
    gather_edges(gather_fine, fine_edge, size_y, fine_cols, False)
    for group in range(planes // ALONG):
        rows = slice(group * ALONG * depth, (group * ALONG + ALONG + 2) * depth)
        held = slice(group * ALONG * chans, (group + 1) * ALONG * chans)
        out = slice(group * ALONG // 2 * chans, (group + 1) * ALONG // 2 * chans)
        for step in range(steps):
            lanes = slice(step * wide, (step + 1) * wide)
            pre = dot(fine_taps_ref[...], fine_cols[rows, lanes])
            mask = fine_mask_ref[:, lanes]
            sigma = sigmoid(pre)
            hidden = (pre * sigma * mask).astype(BF16)
            hidden_ref[held, lanes] = hidden
            slope_ref[held, lanes] = sigma * (1.0 + pre * (1.0 - sigma)) * mask
            pooled = sum_pairs(dot(hidden, pool_ref[...]), chans) * 0.125
            pooled_ref[out, step * size_y : (step + 1) * size_y] = pooled.astype(BF16)
        if group == 0:
            start_downward(1, pooled_ref, pooled_edge)
    start_upward(1, pooled_ref, pooled_edge)

    gather_inner(gather_coarse, pooled_ref, chans, half_y, coarse_cols, False)
    lift_high, lift_low = halves(lift_ref[...])
    up = up_ref[...]
    lifted_grads = []
    for x in range(half):
        held = slice(x * chans, (x + 1) * chans)
        lifted_grads.append(dot_tn(up, lift_high[held]) + dot_tn(up, lift_low[held]))
    grad_hidden = jnp.concatenate(lifted_grads, axis=0)
    finish_edges(1, pooled_ref, pooled_edge)
    gather_edges(gather_coarse, pooled_edge, half_y, coarse_cols, False)
    pre = dot(coarse_taps_ref[...], coarse_cols[...])
    mask = coarse_mask_ref[...]
    sigma = sigmoid(pre)
    slope = sigma * (1.0 + pre * (1.0 - sigma))
    grad_inner_ref[...] = (grad_hidden * mask * slope).astype(BF16)
    start_downward(2, grad_inner_ref, inner_edge)
    start_upward(2, grad_inner_ref, inner_edge)
    inner_ref[...] = (pre * sigma * mask).astype(BF16)
    gather_inner(gather_coarse, grad_inner_ref, inner, half_y, inner_cols, True)

    lifted = jnp.concatenate(
        [dot(up, inner_ref[x * inner : (x + 1) * inner, :]) for x in range(half)], axis=0
    )
    high, low = halves(lifted)
    for step in range(steps):
        lanes = slice(step * wide, (step + 1) * wide)
        coarse = slice(step * size_y, (step + 1) * size_y)
        spread = dot(high[:, coarse], spread_ref[...]) + dot(low[:, coarse], spread_ref[...])
        value = hidden_ref[:, lanes].astype(F32) + fine_mask_ref[:, lanes] * repeat_pairs(
            spread, chans
        )
        net_ref[:, lanes] = value.astype(BF16)
    grad_coarse = 0.0
    grad_up = 0.0
    for x in range(half):
        hidden = inner_ref[x * inner : (x + 1) * inner, :]
        held = slice(x * chans, (x + 1) * chans)
        grad_up += dot_nt(lift_high[held], hidden) + dot_nt(lift_low[held], hidden)
        grad_coarse += dot_nt(
            coarse_cols[x * depth : (x + 3) * depth, :],
            grad_inner_ref[x * inner : (x + 1) * inner, :],
        )
    split = 3 * depth // 2
    packed = inner_sum[0]
    fill = packed.shape[0] - split - chans
    packed[...] = jnp.concatenate(
        [
            jnp.concatenate([grad_coarse[:split], grad_coarse[split:]], axis=1),
            jnp.concatenate([grad_up, jnp.zeros_like(grad_up)], axis=1),
            jnp.zeros((fill, 2 * inner), F32),
        ],
        axis=0,
    ).astype(BF16)
    start(scatter, inner_sum)

    finish_edges(2, grad_inner_ref, inner_edge)
    gather_edges(gather_coarse, inner_edge, half_y, inner_cols, True)
    high, low = halves(dot(coarse_back_ref[...], inner_cols[...]) * 0.125)
    for step in range(steps):
        lanes = slice(step * wide, (step + 1) * wide)
        coarse = slice(step * size_y, (step + 1) * size_y)
        spread = dot(high[:, coarse], spread_ref[...]) + dot(low[:, coarse], spread_ref[...])
        value = cotangent_ref[:, lanes].astype(F32) + repeat_pairs(spread, chans)
        grad_pre_ref[:, lanes] = (value * slope_ref[:, lanes]).astype(BF16)
    start_downward(3, grad_pre_ref, grad_edge)
    start_upward(3, grad_pre_ref, grad_edge)

    gather_inner(gather_fine, grad_pre_ref, chans, size_y, fine_cols, True)
    add_up(inner_sum)

    def taps_of(plane):
        return dot_nt(
            fine_cols[plane * depth : (plane + 1) * depth, :],
            framed[plane * chans : (plane + 3) * chans, :],
        )

    grad_fine = 0.0
    for plane in range(1, planes + 1):
        grad_fine += taps_of(plane)
    finish_edges(3, grad_pre_ref, grad_edge)
    gather_edges(gather_fine, grad_edge, size_y, fine_cols, True)
    grad_fine += taps_of(0) + taps_of(planes + 1)
    tall = 3 * depth // 4
    short = depth - tall
    packed = fine_sum[0]
    rest = jnp.concatenate(
        [grad_fine[tall:, i * chans : (i + 1) * chans] for i in range(3)], axis=0
    )
    packed[...] = jnp.concatenate(
        [
            jnp.concatenate([grad_fine[:tall], rest], axis=1),
            jnp.zeros((packed.shape[0] - tall, 4 * chans), F32),
        ],
        axis=0,
    ).astype(BF16)

    def features_grad(group):
        rows = slice(group * ALONG * depth, (group * ALONG + ALONG + 2) * depth)
        held = slice(group * ALONG * chans, (group + 1) * ALONG * chans)
        for step in range(steps):
            lanes = slice(step * wide, (step + 1) * wide)
            grad_rows_ref[held, lanes] = dot(fine_back_ref[...], fine_cols[rows, lanes])

    start(scatter, fine_sum)
    groups = planes // ALONG
    for group in range(groups // 2):
        features_grad(group)
    add_up(fine_sum)
    for group in range(groups // 2, groups):
        features_grad(group)
    sums = finish(inner_sum)
    grad_coarse_ref[:split, :] = sums[:split, :inner]
    grad_coarse_ref[split:, :] = sums[:split, inner : 2 * inner]
    grad_up_ref[...] = sums[split : split + chans, :inner]
    sums = finish(fine_sum)
    for i in range(3):
        row = i * depth
        grad_fine_ref[row : row + tall, :] = sums[:tall, i * chans : (i + 1) * chans]
        grad_fine_ref[row + tall : row + depth, :] = sums[
            i * short : (i + 1) * short, 3 * chans : 4 * chans
        ]


def banded(flat):
    depth = flat.shape[1] // 3
    return jnp.concatenate(
        [jnp.pad(flat, ((0, 0), (x * depth, (ALONG - 1 - x) * depth))) for x in range(ALONG)],
        axis=0,
    )


def forward_taps(weight):
    outs, ins = weight.shape[:2]
    return banded(weight.transpose(0, 2, 3, 4, 1).reshape(outs, 27 * ins))


def backward_taps(weight):
    outs, ins = weight.shape[:2]
    taps = weight.transpose(1, 2, 3, 4, 0).reshape(ins, 3, 9 * outs)
    return banded(jnp.concatenate([taps[:, i] for i in (2, 1, 0)], axis=1))


def planes_first(values):
    chans, size_x, size_z, size_y = values.shape
    return values.transpose(1, 0, 2, 3).reshape(size_x * chans, size_z * size_y)


def channels_first(values, chans, size_z, size_y):
    return values.reshape(-1, chans, size_z, size_y).transpose(1, 0, 2, 3)


def expand_row(blocks, times):
    values = blocks.astype(F32)[0]
    size_z, size_y = values.shape
    values = jnp.broadcast_to(values[:, None, :, None], (size_z, times, size_y, times))
    return values.reshape(1, size_z * times * size_y * times)


def per_device(features, active_blocks, weight_fine, weight_coarse, weight_up, cotangent):
    chans, size_x, size_z, size_y = features.shape
    inner = weight_coarse.shape[0]
    count = lax.axis_size("gx")
    factor = 1.0 / math.sqrt(size_x * count * size_z * size_y)
    length = size_z * size_y
    half_x, coarse_length = size_x // 2, length // 4

    def sum_scratch(rows, lanes):
        chunk = -(-rows // (16 * count)) * 16
        return (
            pltpu.VMEM((count * chunk, lanes), BF16),
            pltpu.VMEM((count, chunk, lanes), BF16),
            pltpu.VMEM((chunk, lanes), BF16),
            pltpu.VMEM((count * chunk, lanes), BF16),
        ) + (pltpu.SemaphoreType.DMA((count,)),) * 4

    shape = jax.ShapeDtypeStruct
    args = (
        planes_first(features),
        planes_first(cotangent),
        expand_row(active_blocks, 8),
        expand_row(active_blocks, 4),
        jnp.asarray(pool_matrix(size_y), BF16),
        jnp.asarray(pool_matrix(size_y).T, BF16),
        forward_taps(weight_fine),
        forward_taps(weight_coarse),
        backward_taps(weight_coarse),
        backward_taps(weight_fine),
        weight_up,
    )
    out_shape = (
        shape((size_x * chans, length), BF16),
        shape((size_x * chans, length), F32),
        shape((27 * chans, chans), F32),
        shape((27 * chans, inner), F32),
        shape((chans, inner), F32),
    )
    scratch = [
        pltpu.VMEM(((size_x + 2) * 9 * chans, length), BF16),
        pltpu.VMEM(((half_x + 2) * 9 * chans, coarse_length), BF16),
        pltpu.VMEM(((half_x + 2) * 9 * inner, coarse_length), BF16),
        pltpu.VMEM((size_x * chans, length), BF16),
        pltpu.VMEM((size_x * chans, length), F32),
        pltpu.VMEM((half_x * chans, coarse_length), BF16),
        pltpu.VMEM((half_x * inner, coarse_length), BF16),
        pltpu.VMEM((half_x * inner, coarse_length), BF16),
        pltpu.VMEM((size_x * chans, length), BF16),
        pltpu.VMEM((half_x * chans, coarse_length), F32),
        pltpu.VMEM(((size_x + 4) * chans, length), BF16),
        pltpu.VMEM((2, chans, length), BF16),
        pltpu.VMEM((2, chans, coarse_length), BF16),
        pltpu.VMEM((2, inner, coarse_length), BF16),
        pltpu.VMEM((2, chans, length), BF16),
        sum_scratch(27 * chans // 2 + chans, 2 * inner),
        sum_scratch(27 * chans // 4, 4 * chans),
    ]
    scratch += [pltpu.SemaphoreType.DMA((4,))] * 4
    net_rows, grad_rows, grad_fine, grad_coarse, grad_up = pl.pallas_call(
        functools.partial(whole_step, count, factor, size_y),
        out_shape=out_shape,
        in_specs=[pl.BlockSpec(memory_space=pltpu.VMEM)] * len(args),
        out_specs=tuple(pl.BlockSpec(memory_space=pltpu.VMEM) for _ in out_shape),
        scratch_shapes=scratch,
        compiler_params=pltpu.CompilerParams(
            vmem_limit_bytes=VMEM_LIMIT, collective_id=0, has_side_effects=True
        ),
    )(*args)
    taps = (3, 3, 3)
    return (
        channels_first(net_rows, chans, size_z, size_y),
        channels_first(grad_rows, chans, size_z, size_y),
        grad_fine.reshape(taps + (chans, chans)).transpose(3, 4, 0, 1, 2),
        grad_coarse.reshape(taps + (chans, inner)).transpose(4, 3, 0, 1, 2),
        grad_up,
    )


def solution(mesh):
    return jax.shard_map(
        per_device,
        mesh=mesh,
        in_specs=(
            P(None, ("groups", "gx"), None, None),
            P(("groups", "gx"), None, None),
            P(),
            P(),
            P(),
            P(None, ("groups", "gx"), None, None),
        ),
        out_specs=(
            P(None, ("groups", "gx"), None, None),
            P(None, ("groups", "gx"), None, None),
            P("groups", None, None, None, None),
            P("groups", None, None, None, None),
            P("groups", None),
        ),
        check_vma=False,
    )
```

```python
import functools
import math

import jax
import jax.numpy as jnp
import numpy as np
from jax import lax
from jax.experimental import pallas as pl
from jax.experimental.pallas import tpu as pltpu
from jax.sharding import PartitionSpec as P

F32 = jnp.float32
BF16 = jnp.bfloat16
VMEM_LIMIT = 48 * 1024 * 1024
MESH = pl.DeviceIdType.MESH
ALONG = 4


def dot(a, b):
    return jnp.dot(a, b, preferred_element_type=F32)


def dot_nt(a, b):
    return lax.dot_general(a, b, (((1,), (1,)), ((), ())), preferred_element_type=F32)


def dot_tn(a, b):
    return lax.dot_general(a, b, (((0,), (0,)), ((), ())), preferred_element_type=F32)


def halves(value):
    high = value.astype(BF16)
    return high, (value - high.astype(F32)).astype(BF16)


def pool_matrix(size_y):
    cell = np.arange(4 * size_y)
    coarse = np.arange(size_y)
    same_z = (cell // size_y // 2)[:, None] == (coarse // (size_y // 2))[None]
    same_y = (cell % size_y // 2)[:, None] == (coarse % (size_y // 2))[None]
    return (same_z & same_y).astype(np.float32)


def gather_fine(value, size_y, cols_ref, row, reverse):
    chans, length = value.shape
    wide = value.astype(F32)
    spot = lax.broadcasted_iota(jnp.int32, (chans, length), 1) % size_y
    before = jnp.where(spot == 0, 0.0, pltpu.roll(wide, 1, 1)).astype(BF16)
    after = jnp.where(spot == size_y - 1, 0.0, pltpu.roll(wide, length - 1, 1)).astype(BF16)
    edge = jnp.zeros((chans, size_y), BF16)
    blocks = (after, value, before) if reverse else (before, value, after)
    for k, shifted in enumerate(blocks):
        low = pl.ds(row + (k + (6 if reverse else 0)) * chans, chans)
        mid = pl.ds(row + (3 + k) * chans, chans)
        high = pl.ds(row + (k + (0 if reverse else 6)) * chans, chans)
        cols_ref[low, :size_y] = edge
        cols_ref[low, size_y:] = shifted[:, :-size_y]
        cols_ref[mid, :] = shifted
        cols_ref[high, : length - size_y] = shifted[:, size_y:]
        cols_ref[high, length - size_y :] = edge


def gather_coarse(value, size_y, cols_ref, row, reverse):
    chans, length = value.shape
    wide = value.astype(F32)
    cell = lax.broadcasted_iota(jnp.int32, (chans, length), 1)
    spot = cell % size_y
    for j in range(3):
        for k in range(3):
            shift = (j - 1) * size_y + (k - 1)
            rolled = pltpu.roll(wide, (-shift) % length, 1) if shift else wide
            if k == 0:
                rolled = jnp.where(spot == 0, 0.0, rolled)
            if k == 2:
                rolled = jnp.where(spot == size_y - 1, 0.0, rolled)
            if j == 0:
                rolled = jnp.where(cell < size_y, 0.0, rolled)
            if j == 2:
                rolled = jnp.where(cell >= length - size_y, 0.0, rolled)
            tap = 3 * j + k
            block = 8 - tap if reverse else tap
            cols_ref[pl.ds(row + block * chans, chans), :] = rolled.astype(BF16)


def gather_inner(gather, mid_ref, chans, size_y, cols_ref, reverse):
    depth = 9 * chans

    def body(plane, carry):
        start = pl.multiple_of(plane * chans, chans)
        row = pl.multiple_of((plane + 1) * depth, depth)
        gather(mid_ref[pl.ds(start, chans), :], size_y, cols_ref, row, reverse)
        return carry

    lax.fori_loop(0, mid_ref.shape[0] // chans, body, 0)


def gather_edges(gather, edge_ref, size_y, cols_ref, reverse):
    last = cols_ref.shape[0] - 9 * edge_ref.shape[1]
    gather(edge_ref[0], size_y, cols_ref, 0, reverse)
    gather(edge_ref[1], size_y, cols_ref, last, reverse)


def sum_pairs(value, chans):
    count = value.shape[0] // chans
    return jnp.concatenate(
        [
            value[(2 * i) * chans : (2 * i + 1) * chans]
            + value[(2 * i + 1) * chans : (2 * i + 2) * chans]
            for i in range(count // 2)
        ],
        axis=0,
    )


def repeat_pairs(value, chans):
    count = value.shape[0] // chans
    parts = [value[i // 2 * chans : (i // 2 + 1) * chans] for i in range(2 * count)]
    return jnp.concatenate(parts, axis=0)


def sigmoid(value):
    return 1.0 / (1.0 + jnp.exp(-value))


def near_count(count):
    return 4 if count % 4 == 0 else 1


def whole_step(
    count, factor, size_y,
    rows_ref, cotangent_ref, fine_mask_ref, coarse_mask_ref, pool_ref, spread_ref,
    fine_taps_ref, coarse_taps_ref, coarse_back_ref, fine_back_ref, up_ref,
    net_ref, grad_rows_ref, grad_fine_ref, grad_coarse_ref, grad_up_ref,
    fine_cols, coarse_cols, inner_cols, hidden_ref, slope_ref, pooled_ref, inner_ref, grad_inner_ref,
    grad_pre_ref, lift_ref, framed, fine_edge, pooled_edge, inner_edge, grad_edge,
    inner_sum, fine_sum,
    send_low, recv_low, send_high, recv_high,
):
    me = lax.axis_index("gx")
    out_chans, inner = up_ref.shape
    chans = out_chans
    planes = rows_ref.shape[0] // chans
    half = planes // 2
    length = rows_ref.shape[1]
    depth = 9 * chans
    wide = 4 * size_y
    steps = length // wide
    half_y = size_y // 2
    barrier = pltpu.get_barrier_semaphore()

    def peer(d):
        return lax.rem(me + d, count)

    def greet(d, carry):
        pl.semaphore_signal(barrier, inc=1, device_id={"gx": peer(d)}, device_id_type=MESH)
        return carry

    lax.fori_loop(1, count, greet, 0)

    fan = near_count(count)
    outer = count // fan
    spot, group_of = me % fan, me // fan

    def near(d):
        return group_of * fan + lax.rem(spot + d, fan)

    def far(d):
        return lax.rem(me + d * fan, count)

    def rows_of(index, size):
        return pl.ds(pl.multiple_of(index * size, size), size)

    def remote(source, target, send, recv, device):
        return pltpu.make_async_remote_copy(
            src_ref=source,
            dst_ref=target,
            send_sem=send,
            recv_sem=recv,
            device_id={"gx": device},
            device_id_type=MESH,
        )

    def stage_copy(refs, stage, d):
        packed, near_slots, near_part, far_slots, far_part, near_whole, whole = refs[:7]
        send, recv = refs[7 + 2 * stage].at[d], refs[8 + 2 * stage].at[d]
        block, chunk = near_part.shape[0], far_part.shape[0]
        if stage == 0:
            source = packed.at[rows_of(near(d) % fan, block)]
            return remote(source, near_slots.at[d], send, recv, near(d))
        if stage == 1:
            source = near_part.at[rows_of(far(d) // fan, chunk)]
            return remote(source, far_slots.at[d], send, recv, far(d))
        if stage == 2:
            target = near_whole.at[rows_of(group_of, chunk)]
            return remote(far_part, target, send, recv, far(d))
        return remote(near_whole, whole.at[rows_of(spot, block)], send, recv, near(d))

    def each(stage, body, init):
        return lax.fori_loop(1, outer if stage in (1, 2) else fan, body, init)

    def start_stage(refs, stage):
        packed, near_slots, near_part, far_slots, far_part, near_whole, whole = refs[:7]
        block, chunk = near_part.shape[0], far_part.shape[0]

        def added(slots):
            def body(d, total):
                stage_copy(refs, stage - 1, d).wait_recv()
                return total + slots[d].astype(F32)

            return body

        def received(d, carry):
            stage_copy(refs, stage - 1, d).wait_recv()
            return carry

        def begin(d, carry):
            stage_copy(refs, stage, d).start()
            return carry

        if stage == 1:
            first = packed[rows_of(spot, block), :].astype(F32)
            near_part[...] = each(0, added(near_slots), first).astype(BF16)
        if stage == 2:
            first = near_part[rows_of(group_of, chunk), :].astype(F32)
            far_part[...] = (each(1, added(far_slots), first) * factor).astype(BF16)
        if stage == 3:
            near_whole[rows_of(group_of, chunk), :] = far_part[...]
            each(2, received, 0)
        each(stage, begin, 0)

    def finish(refs):
        near_part, near_whole, whole = refs[2], refs[5], refs[6]
        whole[rows_of(spot, near_part.shape[0]), :] = near_whole[...]
        for stage in range(4):

            def body(d, carry, stage=stage):
                stage_copy(refs, stage, d).wait_send()
                if stage == 3:
                    stage_copy(refs, stage, d).wait_recv()
                return carry

            each(stage, body, 0)
        return whole[...].astype(F32)

    def upward(index, values_ref, edge_ref):
        size = edge_ref.shape[1]
        return pltpu.make_async_remote_copy(
            src_ref=values_ref.at[pl.ds(values_ref.shape[0] - size, size)],
            dst_ref=edge_ref.at[0],
            send_sem=send_low.at[index],
            recv_sem=recv_low.at[index],
            device_id={"gx": lax.rem(me + 1, count)},
            device_id_type=MESH,
        )

    def downward(index, values_ref, edge_ref):
        size = edge_ref.shape[1]
        return pltpu.make_async_remote_copy(
            src_ref=values_ref.at[pl.ds(0, size)],
            dst_ref=edge_ref.at[1],
            send_sem=send_high.at[index],
            recv_sem=recv_high.at[index],
            device_id={"gx": lax.rem(me + count - 1, count)},
            device_id_type=MESH,
        )

    def start_upward(*args):
        @pl.when(me < count - 1)
        def _():
            upward(*args).start()

    def start_downward(*args):
        @pl.when(me > 0)
        def _():
            downward(*args).start()

    def finish_edges(*args):
        edge_ref = args[2]

        @pl.when(me > 0)
        def _():
            upward(*args).wait_recv()
            downward(*args).wait_send()

        @pl.when(me == 0)
        def _():
            edge_ref[0] = jnp.zeros(edge_ref.shape[1:], BF16)

        @pl.when(me < count - 1)
        def _():
            downward(*args).wait_recv()
            upward(*args).wait_send()

        @pl.when(me == count - 1)
        def _():
            edge_ref[1] = jnp.zeros(edge_ref.shape[1:], BF16)

    for step in range(steps):
        lanes = slice(step * wide, (step + 1) * wide)
        value = (cotangent_ref[:, lanes].astype(F32) * fine_mask_ref[:, lanes]).astype(BF16)
        lift_ref[:, step * size_y : (step + 1) * size_y] = sum_pairs(
            dot(value, pool_ref[...]), chans
        )
    empty = jnp.zeros((2 * chans, length), BF16)
    framed[: 2 * chans, :] = empty
    framed[2 * chans : (planes + 2) * chans, :] = rows_ref[...]
    framed[(planes + 2) * chans :, :] = empty

    pl.semaphore_wait(barrier, count - 1)
    start_upward(0, rows_ref, fine_edge)
    start_downward(0, rows_ref, fine_edge)
    gather_inner(gather_fine, rows_ref, chans, size_y, fine_cols, False)
    finish_edges(0, rows_ref, fine_edge)
    gather_edges(gather_fine, fine_edge, size_y, fine_cols, False)
    for group in range(planes // ALONG):
        rows = slice(group * ALONG * depth, (group * ALONG + ALONG + 2) * depth)
        held = slice(group * ALONG * chans, (group + 1) * ALONG * chans)
        out = slice(group * ALONG // 2 * chans, (group + 1) * ALONG // 2 * chans)
        for step in range(steps):
            lanes = slice(step * wide, (step + 1) * wide)
            pre = dot(fine_taps_ref[...], fine_cols[rows, lanes])
            mask = fine_mask_ref[:, lanes]
            sigma = sigmoid(pre)
            hidden = (pre * sigma * mask).astype(BF16)
            hidden_ref[held, lanes] = hidden
            slope_ref[held, lanes] = sigma * (1.0 + pre * (1.0 - sigma)) * mask
            pooled = sum_pairs(dot(hidden, pool_ref[...]), chans) * 0.125
            pooled_ref[out, step * size_y : (step + 1) * size_y] = pooled.astype(BF16)
        if group == 0:
            start_downward(1, pooled_ref, pooled_edge)
    start_upward(1, pooled_ref, pooled_edge)

    gather_inner(gather_coarse, pooled_ref, chans, half_y, coarse_cols, False)
    lift_high, lift_low = halves(lift_ref[...])
    up = up_ref[...]
    lifted_grads = []
    for x in range(half):
        held = slice(x * chans, (x + 1) * chans)
        lifted_grads.append(dot_tn(up, lift_high[held]) + dot_tn(up, lift_low[held]))
    grad_hidden = jnp.concatenate(lifted_grads, axis=0)
    finish_edges(1, pooled_ref, pooled_edge)
    gather_edges(gather_coarse, pooled_edge, half_y, coarse_cols, False)
    pre = dot(coarse_taps_ref[...], coarse_cols[...])
    mask = coarse_mask_ref[...]
    sigma = sigmoid(pre)
    slope = sigma * (1.0 + pre * (1.0 - sigma))
    grad_inner_ref[...] = (grad_hidden * mask * slope).astype(BF16)
    start_downward(2, grad_inner_ref, inner_edge)
    start_upward(2, grad_inner_ref, inner_edge)
    inner_ref[...] = (pre * sigma * mask).astype(BF16)
    gather_inner(gather_coarse, grad_inner_ref, inner, half_y, inner_cols, True)

    lifted = jnp.concatenate(
        [dot(up, inner_ref[x * inner : (x + 1) * inner, :]) for x in range(half)], axis=0
    )
    high, low = halves(lifted)
    for step in range(steps):
        lanes = slice(step * wide, (step + 1) * wide)
        coarse = slice(step * size_y, (step + 1) * size_y)
        spread = dot(high[:, coarse], spread_ref[...]) + dot(low[:, coarse], spread_ref[...])
        value = hidden_ref[:, lanes].astype(F32) + fine_mask_ref[:, lanes] * repeat_pairs(
            spread, chans
        )
        net_ref[:, lanes] = value.astype(BF16)
    grad_coarse = 0.0
    grad_up = 0.0
    for x in range(half):
        hidden = inner_ref[x * inner : (x + 1) * inner, :]
        held = slice(x * chans, (x + 1) * chans)
        grad_up += dot_nt(lift_high[held], hidden) + dot_nt(lift_low[held], hidden)
        grad_coarse += dot_nt(
            coarse_cols[x * depth : (x + 3) * depth, :],
            grad_inner_ref[x * inner : (x + 1) * inner, :],
        )
    split = 3 * depth // 2
    packed = inner_sum[0]
    fill = packed.shape[0] - split - chans
    packed[...] = jnp.concatenate(
        [
            jnp.concatenate([grad_coarse[:split], grad_coarse[split:]], axis=1),
            jnp.concatenate([grad_up, jnp.zeros_like(grad_up)], axis=1),
            jnp.zeros((fill, 2 * inner), F32),
        ],
        axis=0,
    ).astype(BF16)
    start_stage(inner_sum, 0)

    finish_edges(2, grad_inner_ref, inner_edge)
    gather_edges(gather_coarse, inner_edge, half_y, inner_cols, True)
    start_stage(inner_sum, 1)
    high, low = halves(dot(coarse_back_ref[...], inner_cols[...]) * 0.125)
    for step in range(steps):
        lanes = slice(step * wide, (step + 1) * wide)
        coarse = slice(step * size_y, (step + 1) * size_y)
        spread = dot(high[:, coarse], spread_ref[...]) + dot(low[:, coarse], spread_ref[...])
        value = cotangent_ref[:, lanes].astype(F32) + repeat_pairs(spread, chans)
        grad_pre_ref[:, lanes] = (value * slope_ref[:, lanes]).astype(BF16)
    start_downward(3, grad_pre_ref, grad_edge)
    start_upward(3, grad_pre_ref, grad_edge)

    gather_inner(gather_fine, grad_pre_ref, chans, size_y, fine_cols, True)
    start_stage(inner_sum, 2)

    def taps_of(plane):
        return dot_nt(
            fine_cols[plane * depth : (plane + 1) * depth, :],
            framed[plane * chans : (plane + 3) * chans, :],
        )

    grad_fine = 0.0
    for plane in range(1, planes + 1):
        grad_fine += taps_of(plane)
    finish_edges(3, grad_pre_ref, grad_edge)
    gather_edges(gather_fine, grad_edge, size_y, fine_cols, True)
    start_stage(inner_sum, 3)
    grad_fine += taps_of(0) + taps_of(planes + 1)
    tall = 3 * depth // 4
    short = depth - tall
    packed = fine_sum[0]
    rest = jnp.concatenate(
        [grad_fine[tall:, i * chans : (i + 1) * chans] for i in range(3)], axis=0
    )
    packed[...] = jnp.concatenate(
        [
            jnp.concatenate([grad_fine[:tall], rest], axis=1),
            jnp.zeros((packed.shape[0] - tall, 4 * chans), F32),
        ],
        axis=0,
    ).astype(BF16)

    start_stage(fine_sum, 0)
    work = [(group, step) for group in range(planes // ALONG) for step in range(steps)]
    for index, (group, step) in enumerate(work):
        rows = slice(group * ALONG * depth, (group * ALONG + ALONG + 2) * depth)
        held = slice(group * ALONG * chans, (group + 1) * ALONG * chans)
        lanes = slice(step * wide, (step + 1) * wide)
        grad_rows_ref[held, lanes] = dot(fine_back_ref[...], fine_cols[rows, lanes])
        for stage in (1, 2, 3):
            if index == stage * len(work) // 4 - 1:
                start_stage(fine_sum, stage)
    sums = finish(inner_sum)
    grad_coarse_ref[:split, :] = sums[:split, :inner]
    grad_coarse_ref[split:, :] = sums[:split, inner : 2 * inner]
    grad_up_ref[...] = sums[split : split + chans, :inner]
    sums = finish(fine_sum)
    for i in range(3):
        row = i * depth
        grad_fine_ref[row : row + tall, :] = sums[:tall, i * chans : (i + 1) * chans]
        grad_fine_ref[row + tall : row + depth, :] = sums[
            i * short : (i + 1) * short, 3 * chans : 4 * chans
        ]


def banded(flat):
    depth = flat.shape[1] // 3
    return jnp.concatenate(
        [jnp.pad(flat, ((0, 0), (x * depth, (ALONG - 1 - x) * depth))) for x in range(ALONG)],
        axis=0,
    )


def forward_taps(weight):
    outs, ins = weight.shape[:2]
    return banded(weight.transpose(0, 2, 3, 4, 1).reshape(outs, 27 * ins))


def backward_taps(weight):
    outs, ins = weight.shape[:2]
    taps = weight.transpose(1, 2, 3, 4, 0).reshape(ins, 3, 9 * outs)
    return banded(jnp.concatenate([taps[:, i] for i in (2, 1, 0)], axis=1))


def planes_first(values):
    chans, size_x, size_z, size_y = values.shape
    return values.transpose(1, 0, 2, 3).reshape(size_x * chans, size_z * size_y)


def channels_first(values, chans, size_z, size_y):
    return values.reshape(-1, chans, size_z, size_y).transpose(1, 0, 2, 3)


def expand_row(blocks, times):
    values = blocks.astype(F32)[0]
    size_z, size_y = values.shape
    values = jnp.broadcast_to(values[:, None, :, None], (size_z, times, size_y, times))
    return values.reshape(1, size_z * times * size_y * times)


def per_device(features, active_blocks, weight_fine, weight_coarse, weight_up, cotangent):
    chans, size_x, size_z, size_y = features.shape
    inner = weight_coarse.shape[0]
    count = lax.axis_size("gx")
    factor = 1.0 / math.sqrt(size_x * count * size_z * size_y)
    length = size_z * size_y
    half_x, coarse_length = size_x // 2, length // 4

    def sum_scratch(rows, lanes):
        chunk = -(-rows // (16 * count)) * 16
        fan = near_count(count)
        outer = count // fan
        near, far = pltpu.SemaphoreType.DMA((fan,)), pltpu.SemaphoreType.DMA((outer,))
        return (
            pltpu.VMEM((count * chunk, lanes), BF16),
            pltpu.VMEM((fan, outer * chunk, lanes), BF16),
            pltpu.VMEM((outer * chunk, lanes), BF16),
            pltpu.VMEM((outer, chunk, lanes), BF16),
            pltpu.VMEM((chunk, lanes), BF16),
            pltpu.VMEM((outer * chunk, lanes), BF16),
            pltpu.VMEM((count * chunk, lanes), BF16),
        ) + (near, near, far, far, far, far, near, near)

    shape = jax.ShapeDtypeStruct
    args = (
        planes_first(features),
        planes_first(cotangent),
        expand_row(active_blocks, 8),
        expand_row(active_blocks, 4),
        jnp.asarray(pool_matrix(size_y), BF16),
        jnp.asarray(pool_matrix(size_y).T, BF16),
        forward_taps(weight_fine),
        forward_taps(weight_coarse),
        backward_taps(weight_coarse),
        backward_taps(weight_fine),
        weight_up,
    )
    out_shape = (
        shape((size_x * chans, length), BF16),
        shape((size_x * chans, length), F32),
        shape((27 * chans, chans), F32),
        shape((27 * chans, inner), F32),
        shape((chans, inner), F32),
    )
    scratch = [
        pltpu.VMEM(((size_x + 2) * 9 * chans, length), BF16),
        pltpu.VMEM(((half_x + 2) * 9 * chans, coarse_length), BF16),
        pltpu.VMEM(((half_x + 2) * 9 * inner, coarse_length), BF16),
        pltpu.VMEM((size_x * chans, length), BF16),
        pltpu.VMEM((size_x * chans, length), F32),
        pltpu.VMEM((half_x * chans, coarse_length), BF16),
        pltpu.VMEM((half_x * inner, coarse_length), BF16),
        pltpu.VMEM((half_x * inner, coarse_length), BF16),
        pltpu.VMEM((size_x * chans, length), BF16),
        pltpu.VMEM((half_x * chans, coarse_length), F32),
        pltpu.VMEM(((size_x + 4) * chans, length), BF16),
        pltpu.VMEM((2, chans, length), BF16),
        pltpu.VMEM((2, chans, coarse_length), BF16),
        pltpu.VMEM((2, inner, coarse_length), BF16),
        pltpu.VMEM((2, chans, length), BF16),
        sum_scratch(27 * chans // 2 + chans, 2 * inner),
        sum_scratch(27 * chans // 4, 4 * chans),
    ]
    scratch += [pltpu.SemaphoreType.DMA((4,))] * 4
    net_rows, grad_rows, grad_fine, grad_coarse, grad_up = pl.pallas_call(
        functools.partial(whole_step, count, factor, size_y),
        out_shape=out_shape,
        in_specs=[pl.BlockSpec(memory_space=pltpu.VMEM)] * len(args),
        out_specs=tuple(pl.BlockSpec(memory_space=pltpu.VMEM) for _ in out_shape),
        scratch_shapes=scratch,
        compiler_params=pltpu.CompilerParams(
            vmem_limit_bytes=VMEM_LIMIT, collective_id=0, has_side_effects=True
        ),
    )(*args)
    taps = (3, 3, 3)
    return (
        channels_first(net_rows, chans, size_z, size_y),
        channels_first(grad_rows, chans, size_z, size_y),
        grad_fine.reshape(taps + (chans, chans)).transpose(3, 4, 0, 1, 2),
        grad_coarse.reshape(taps + (chans, inner)).transpose(4, 3, 0, 1, 2),
        grad_up,
    )


def solution(mesh):
    return jax.shard_map(
        per_device,
        mesh=mesh,
        in_specs=(
            P(None, ("groups", "gx"), None, None),
            P(("groups", "gx"), None, None),
            P(),
            P(),
            P(),
            P(None, ("groups", "gx"), None, None),
        ),
        out_specs=(
            P(None, ("groups", "gx"), None, None),
            P(None, ("groups", "gx"), None, None),
            P("groups", None, None, None, None),
            P("groups", None, None, None, None),
            P("groups", None),
        ),
        check_vma=False,
    )
```
